32 devices in a mesh: dp: 16 (over z, y, core), mp: 2 (over x).
Axes of the slice: x: 2, y: 2, z: 4, core: 2. Of those that a mesh axis runs over, the one named last changes fastest.
Arguments:
- latents: bfloat16 [16, 1024, 1024], P('dp', 'mp'), may hold values from -6 to 6
- condition: bfloat16 [16, 1024], P('dp'), may hold values from -6 to 6
- modulation_weight: bfloat16 [1024, 6, 1024], P('dp', None, 'mp'), may hold values from -0.1875 to 0.1875
- modulation_bias: bfloat16 [6, 1024], P(None, ('mp', 'dp')), may hold values from -3 to 3
- query_key_value_weight: bfloat16 [1024, 3, 1024], P('dp', None, 'mp'), may hold values from -0.1875 to 0.1875
- query_value_bias: bfloat16 [2, 1024], P(None, ('mp', 'dp')), may hold values from -3 to 3
- attention_output_weight: bfloat16 [1024, 1024], P('mp', 'dp'), may hold values from -1.5 to 1.5
- up_projection_weight: bfloat16 [1024, 4096], P('dp', 'mp'), may hold values from -0.1875 to 0.1875
- up_projection_bias: bfloat16 [4096], P(('mp', 'dp')), may hold values from -3 to 3
- down_projection_weight: bfloat16 [4096, 1024], P('mp', 'dp'), may hold values from -0.09375 to 0.09375
- projection_row_bias: bfloat16 [2, 1024], P(None, ('mp', 'dp')), may hold values from -3 to 3
- cotangent: bfloat16 [16, 1024, 1024], P('dp', 'mp'), may hold values from -6 to 6
Outputs:
- output: bfloat16 [16, 1024, 1024], P('dp', 'mp')
- latents_grad: bfloat16 [16, 1024, 1024], P('dp', 'mp')
- condition_grad: bfloat16 [16, 1024], P('dp', 'mp')
- mod_weight_grad: float32 [1024, 6, 1024], P('dp', None, 'mp')
- mod_bias_grad: float32 [6, 1024], P(None, ('mp', 'dp'))
- qkv_weight_grad: float32 [1024, 3, 1024], P('dp', None, 'mp')
- qv_bias_grad: float32 [2, 1024], P(None, ('mp', 'dp'))
- out_weight_grad: float32 [1024, 1024], P('mp', 'dp')
- up_weight_grad: float32 [1024, 4096], P('dp', 'mp')
- up_bias_grad: float32 [4096], P(('mp', 'dp'))
- down_weight_grad: float32 [4096, 1024], P('mp', 'dp')
- row_bias_grad: float32 [2, 1024], P(None, ('mp', 'dp'))
The draws below stay inside these ranges and needn't reach their ends.
All inputs are finite; a program needn't handle non-finite values.
Results may differ from the reference program's by a relative error of at most 0.02.
The reference program's roundings to bfloat16 on the way count: a program that leaves them out, or rounds other values in their place, can miss the bound.
Values may be sent and summed in bfloat16 or wider, within the bound.
A program may use at most 192 MiB of HBM per device.

```python
import jax
import jax.numpy as jnp
from jax import lax

HEADS = 16
HEAD_DIM = 64
D = 1024
FF = 4096
SEQ_LEN = 1024
LATENTS = 16


def block_levels(own_key, shape, pieces, least, high):
    level, own = 1.0, jax.random.fold_in(own_key, 6)
    for position, shards_of in pieces:
        draws = jnp.exp(jax.random.uniform(jax.random.fold_in(own, position), (shards_of,), jnp.float32, least / len(pieces), high / len(pieces)))
        level = level * jnp.repeat(draws, shape[position] // shards_of).reshape([-1 if axis == position else 1 for axis in range(len(shape))])
    return level


def bell_draw(own_key, shape, scale, most, shards=(), dtype=jnp.bfloat16):
    factor_of = block_levels(own_key, shape, shards, -0.22, 0.18) if shards else 1.0
    values = jax.random.normal(own_key, shape, jnp.float32) * scale * factor_of
    return jnp.minimum(jnp.maximum(values, -most), most).astype(dtype)


def setup_inputs(seed: int = 0) -> dict:
    keys = jax.random.split(jax.random.key(seed), 13)
    latents = bell_draw(keys[0], (LATENTS, SEQ_LEN, D), 1.0, 6.0, ((0, 16), (1, 2)))
    condition = bell_draw(keys[1], (LATENTS, D), 1.0, 6.0, ((0, 16),))
    modulation_weight = bell_draw(keys[2], (D, 6, D), D ** -0.5, 0.1875, ((0, 16), (2, 2)))
    modulation_bias = bell_draw(keys[3], (6, D), 0.5, 3.0, ((1, 32),))
    query_key_value_weight = bell_draw(keys[4], (D, 3, D), D ** -0.5, 0.1875, ((0, 16), (2, 2)))
    query_value_bias = bell_draw(keys[5], (2, D), 0.5, 3.0, ((1, 32),))
    attention_output_weight = bell_draw(keys[6], (D, D), (D // 64) ** -0.5, 1.5, ((0, 2), (1, 16)))
    up_projection_weight = bell_draw(keys[7], (D, FF), D ** -0.5, 0.1875, ((0, 16), (1, 2)))
    up_projection_bias = bell_draw(keys[8], (FF,), 0.5, 3.0, ((0, 32),))
    down_projection_weight = bell_draw(keys[9], (FF, D), FF ** -0.5, 0.09375, ((0, 2), (1, 16)))
    projection_row_bias = bell_draw(keys[10], (2, D), 0.5, 3.0, ((1, 32),))
    cotangent = bell_draw(keys[11], (LATENTS, SEQ_LEN, D), 1.0, 6.0, ((0, 16), (1, 2)))
    return {"latents": latents, "condition": condition, "modulation_weight": modulation_weight, "modulation_bias": modulation_bias, "query_key_value_weight": query_key_value_weight, "query_value_bias": query_value_bias, "attention_output_weight": attention_output_weight, "up_projection_weight": up_projection_weight, "up_projection_bias": up_projection_bias, "down_projection_weight": down_projection_weight, "projection_row_bias": projection_row_bias, "cotangent": cotangent}


@jax.custom_vjp
def low(v):
    return lax.optimization_barrier(v.astype(jnp.bfloat16)).astype(jnp.float32)

@jax.custom_vjp
def low_back(v):
    return v

def low_keep(v):
    return (low(v), None)

def low_pass(kept, grad):
    return (grad,)

def back_keep(v):
    return (v, None)

def back_low(kept, grad):
    return (low(grad),)
low.defvjp(low_keep, low_pass)
low_back.defvjp(back_keep, back_low)
epsilon = 1e-06
precise = lax.Precision.HIGHEST

def round_both(values):
    return low(low_back(values))

def layer_norm(values):
    center = values - lax.optimization_barrier(jnp.mean(values, axis=-1, keepdims=True))
    return center * lax.rsqrt(lax.optimization_barrier(jnp.mean(center * center, axis=-1, keepdims=True)) + epsilon)

def diffusion_transformer_layer(token_rows, condition_vector, modulation_weight, modulation_bias, query_key_value_weight, query_value_bias, attention_output_weight, up_projection_weight, up_projection_bias, down_projection_weight, projection_row_bias):
    activated = low(jax.nn.silu(condition_vector))
    modulation = jnp.einsum('d,dkf->kf', activated, modulation_weight, precision=precise) + modulation_bias
    input_attn = low(layer_norm(token_rows) * (1.0 + modulation[1]) + modulation[0])
    qkv_shift = jnp.stack([query_value_bias[0], jnp.zeros_like(query_value_bias[0]), query_value_bias[1]])
    qkv_all = round_both(jnp.einsum('td,dkf->tkf', input_attn, query_key_value_weight, precision=precise) + qkv_shift)
    shape_heads = (SEQ_LEN, HEADS, HEAD_DIM)
    queries = qkv_all[:, 0].reshape(shape_heads)
    keys_all = qkv_all[:, 1].reshape(shape_heads)
    values_all = qkv_all[:, 2].reshape(shape_heads)
    scores = low_back(jnp.einsum('qhe,khe->hqk', queries, keys_all, precision=precise) * HEAD_DIM ** (-0.5))
    attention = low(jax.nn.softmax(scores, axis=-1))
    attended = round_both(jnp.einsum('hqk,khe->qhe', attention, values_all, precision=precise))
    attended = attended.reshape(SEQ_LEN, HEADS * HEAD_DIM)
    branch_attn = low_back(jnp.dot(attended, attention_output_weight, precision=precise) + projection_row_bias[0])
    middle = token_rows + modulation[2] * branch_attn
    input_mlp = low(layer_norm(middle) * (1.0 + modulation[4]) + modulation[3])
    pre_up = low_back(jnp.dot(input_mlp, up_projection_weight, precision=precise) + up_projection_bias)
    hidden = low(jax.nn.gelu(pre_up, approximate=True))
    branch_mlp = low_back(jnp.dot(hidden, down_projection_weight, precision=precise) + projection_row_bias[1])
    return middle + modulation[5] * branch_mlp

def reference(latents, condition, modulation_weight, modulation_bias, query_key_value_weight, query_value_bias, attention_output_weight, up_projection_weight, up_projection_bias, down_projection_weight, projection_row_bias, cotangent):
    layer_weights = tuple((element.astype(jnp.float32) for element in (modulation_weight, modulation_bias, query_key_value_weight, query_value_bias, attention_output_weight, up_projection_weight, up_projection_bias, down_projection_weight, projection_row_bias)))

    def one_latent(running, sample):
        token_rows, condition_vector, grad_output = sample
        layer_output, backward_rule = jax.vjp(diffusion_transformer_layer, token_rows.astype(jnp.float32), condition_vector.astype(jnp.float32), *layer_weights)
        gradients = backward_rule(grad_output.astype(jnp.float32))
        running = tuple((previous + contribution for previous, contribution in zip(running, gradients[2:])))
        return (running, (layer_output.astype(jnp.bfloat16), gradients[0].astype(jnp.bfloat16), gradients[1].astype(jnp.bfloat16)))
    initial = tuple((jnp.zeros_like(element) for element in layer_weights))
    totals, (output, latents_grad, condition_grad) = lax.scan(one_latent, initial, (latents, condition, cotangent))
    return (output, latents_grad, condition_grad) + tuple(totals)
```

```python
import jax
import jax.numpy as jnp
from jax import lax
from jax.experimental import pallas as pl
from jax.experimental.pallas import tpu as pltpu
from jax.sharding import PartitionSpec as P

HEAD_DIM = 64
PAIR = 2 * HEAD_DIM
TEMPER = HEAD_DIM ** (-0.5)

epsilon = 1e-06
precise = lax.Precision.HIGHEST
f32 = jnp.float32
bf16 = jnp.bfloat16


def layer_norm(values):
    center = values - jnp.mean(values, axis=-1, keepdims=True)
    inverse = lax.rsqrt(jnp.mean(center * center, axis=-1, keepdims=True) + epsilon)
    return (center * inverse, inverse)


def norm_back(grad_normed, normed, inverse):
    first = jnp.mean(grad_normed, axis=-1, keepdims=True)
    second = jnp.mean(grad_normed * normed, axis=-1, keepdims=True)
    return inverse * (grad_normed - first - normed * second)


def gelu_tanh(values):
    return jax.nn.gelu(values, approximate=True)


def dot(a, b, contract):
    return lax.dot_general(a, b, (contract, ((), ())), preferred_element_type=f32)


def nn(a, b):
    return dot(a, b, ((1,), (0,)))


def nt(a, b):
    return dot(a, b, ((1,), (1,)))


def tn(a, b):
    return dot(a, b, ((0,), (0,)))


def head_columns(ref, part, head, rows=slice(None)):
    start = part * PAIR + head * HEAD_DIM
    return ref[rows, start : start + HEAD_DIM]


def softmax_columns(scores):
    exponent = jnp.exp(scores - jnp.max(scores, axis=0, keepdims=True))
    return exponent * (1.0 / jnp.sum(exponent, axis=0, keepdims=True))


def attend_kernel(block, qkv_ref, out_ref):
    keys = [head_columns(qkv_ref, 1, h) for h in range(2)]
    values_t = [head_columns(qkv_ref, 2, h).T for h in range(2)]
    for first in range(0, qkv_ref.shape[0], block):
        rows = slice(first, first + block)
        parts = []
        for h in range(2):
            query = head_columns(qkv_ref, 0, h, rows) * TEMPER
            probs = softmax_columns(nt(keys[h], query)).astype(bf16)
            parts.append(nn(values_t[h], probs))
        out_ref[rows, :] = jnp.concatenate(parts, axis=0).T.astype(bf16)


def attend_back_kernel(block, qkv_ref, grad_ref, out_ref, grad_key, grad_value):
    keys = [head_columns(qkv_ref, 1, h) for h in range(2)]
    values = [head_columns(qkv_ref, 2, h) for h in range(2)]
    keys_t = [keys[h].T for h in range(2)]
    for first in range(0, qkv_ref.shape[0], block):
        rows = slice(first, first + block)
        parts = []
        for h in range(2):
            query = head_columns(qkv_ref, 0, h, rows) * TEMPER
            grad = grad_ref[rows, h * HEAD_DIM : (h + 1) * HEAD_DIM]
            probs = softmax_columns(nt(keys[h], query))
            grad_probs = nt(values[h], grad)
            inner = jnp.sum(probs * grad_probs, axis=0, keepdims=True)
            grad_scores = (probs * (grad_probs - inner)).astype(bf16)
            value_part = nn(probs.astype(bf16), grad)
            key_part = nn(grad_scores, query)
            if first == 0:
                grad_value[h] = value_part
                grad_key[h] = key_part
            else:
                grad_value[h] += value_part
                grad_key[h] += key_part
            parts.append(nn(keys_t[h], grad_scores))
        out_ref[rows, :PAIR] = (jnp.concatenate(parts, axis=0).T * TEMPER).astype(bf16)
    out_ref[:, PAIR : 2 * PAIR] = jnp.concatenate([grad_key[0], grad_key[1]], axis=1).astype(bf16)
    out_ref[:, 2 * PAIR :] = jnp.concatenate([grad_value[0], grad_value[1]], axis=1).astype(bf16)


def attend(qkv):
    tokens, width = qkv.shape
    pairs = width // (3 * PAIR)
    block = min(256, tokens)

    def body(qkv_ref, out_ref):
        attend_kernel(block, qkv_ref, out_ref)

    return pl.pallas_call(
        body,
        grid=(pairs,),
        in_specs=[pl.BlockSpec((tokens, 3 * PAIR), lambda p: (0, p))],
        out_specs=pl.BlockSpec((tokens, PAIR), lambda p: (0, p)),
        out_shape=jax.ShapeDtypeStruct((tokens, pairs * PAIR), bf16),
        compiler_params=pltpu.CompilerParams(vmem_limit_bytes=40 * 2**20),
        cost_estimate=pl.CostEstimate(
            flops=16 * pairs * tokens * tokens * PAIR,
            bytes_accessed=8 * tokens * pairs * PAIR,
            transcendentals=2 * pairs * tokens * tokens,
        ),
        name="attend",
    )(qkv)


def attend_back(qkv, grad):
    tokens, width = qkv.shape
    pairs = width // (3 * PAIR)
    block = min(256, tokens)

    def body(*refs):
        attend_back_kernel(block, *refs)

    return pl.pallas_call(
        body,
        grid=(pairs,),
        in_specs=[
            pl.BlockSpec((tokens, 3 * PAIR), lambda p: (0, p)),
            pl.BlockSpec((tokens, PAIR), lambda p: (0, p)),
        ],
        out_specs=pl.BlockSpec((tokens, 3 * PAIR), lambda p: (0, p)),
        out_shape=jax.ShapeDtypeStruct((tokens, width), bf16),
        scratch_shapes=[
            pltpu.VMEM((2, tokens, HEAD_DIM), f32),
            pltpu.VMEM((2, tokens, HEAD_DIM), f32),
        ],
        compiler_params=pltpu.CompilerParams(vmem_limit_bytes=40 * 2**20),
        cost_estimate=pl.CostEstimate(
            flops=40 * pairs * tokens * tokens * PAIR,
            bytes_accessed=14 * tokens * pairs * PAIR,
            transcendentals=2 * pairs * tokens * tokens,
        ),
        name="attend_back",
    )(qkv, grad)


def by_pairs(matrix):
    rows, parts, width = matrix.shape
    split = matrix.reshape(rows, parts, width // PAIR, PAIR)
    return jnp.swapaxes(split, 1, 2).reshape(rows, parts * width)


def from_pairs(matrix):
    rows, width = matrix.shape
    split = matrix.reshape(rows, width // (3 * PAIR), 3, PAIR)
    return jnp.swapaxes(split, 1, 2).reshape(rows, 3, width // 3)


def swap(values):
    return lax.ppermute(values, "mp", [(0, 1), (1, 0)])


def expand(values):
    if lax.axis_size("mp") == 2:
        return [values, swap(values)]
    return [lax.all_gather(values, "mp", axis=0, tiled=True)]


def owned_sums(function, chunks):
    if lax.axis_size("mp") == 2:
        received = swap(function(chunks[1]).astype(bf16))
        return function(chunks[0]) + received.astype(f32)
    return lax.psum_scatter(
        function(chunks[0]).astype(bf16), "mp", scatter_dimension=0, tiled=True
    ).astype(f32)


def chunked(values, count):
    return jnp.split(values, count, axis=0) if count > 1 else [values]


def joined(chunks):
    return jnp.concatenate(chunks, axis=0) if len(chunks) > 1 else chunks[0]


def to_latents(values):
    dp, mp = lax.axis_size("dp"), lax.axis_size("mp")
    width = values.shape[1]
    repeated = jnp.broadcast_to(values[:, None], (dp, mp, width)).reshape(dp * mp, width)
    received = lax.all_to_all(repeated, ("dp", "mp"), 0, 0, tiled=True)
    return received.reshape(dp, mp, width)


def local(
    latents,
    condition,
    modulation_weight,
    modulation_bias,
    query_key_value_weight,
    query_value_bias,
    attention_output_weight,
    up_projection_weight,
    up_projection_bias,
    down_projection_weight,
    projection_row_bias,
    cotangent,
):
    mp, dp = lax.axis_size("mp"), lax.axis_size("dp")
    my_dp, my_mp = lax.axis_index("dp"), lax.axis_index("mp")
    model_width = latents.shape[2]
    width = model_width // mp
    rows = model_width // dp
    ff = up_projection_weight.shape[1]
    tokens_in = latents[0].astype(f32)
    grad_out = cotangent[0].astype(f32)
    cond_float = condition.astype(f32)
    activated = jax.nn.silu(cond_float).astype(bf16)

    small_parts = [
        activated,
        modulation_bias.reshape(1, -1),
        query_value_bias.reshape(1, -1),
        up_projection_bias.reshape(1, -1),
        projection_row_bias.reshape(1, -1),
    ]
    bounds = []
    for part in small_parts:
        start = bounds[-1][1] if bounds else 0
        bounds.append((start, start + part.shape[1]))
    small = lax.all_gather(jnp.concatenate(small_parts, axis=1), "dp", axis=0, tiled=True)
    small_out = [small[:, a:b] for a, b in bounds]

    def bias_rows(gathered, count):
        split = gathered.reshape(dp, count, -1)
        return jnp.swapaxes(split, 0, 1).reshape(count, -1).astype(f32)

    mod_offset = bias_rows(small_out[1], 6)
    qv_offset = bias_rows(small_out[2], 2)
    up_offset = bias_rows(small_out[3], 1)
    row_offset = bias_rows(small_out[4], 2)
    act_rows = lax.dynamic_slice_in_dim(small_out[0], my_dp * rows, rows, axis=1)

    qkv_matrix = lax.all_gather(by_pairs(query_key_value_weight), "dp", axis=0, tiled=True)
    packed = jnp.concatenate(
        [attention_output_weight.T, up_projection_weight, down_projection_weight.T], axis=1
    )
    packed_full = lax.all_gather(packed, "dp", axis=0, tiled=True)
    out_matrix_t = packed_full[:, :width]
    up_matrix = packed_full[:, width : width + ff]
    down_matrix_t = packed_full[:, width + ff :]

    mod_flat = modulation_weight.reshape(rows, -1)
    mod_partial = nn(act_rows, mod_flat)
    extra = jnp.concatenate([mod_offset.reshape(1, -1), row_offset.reshape(1, -1)], axis=1)
    payload = jnp.pad(mod_partial, ((0, 0), (0, 2 * width))) + jnp.where(my_dp == 0, extra, 0.0)
    arrived = jnp.sum(to_latents(payload), axis=0).reshape(mp, 8, width)
    vectors = jnp.swapaxes(arrived, 0, 1).reshape(8, 1, model_width)
    shift_attn, scale_attn, gate_attn, shift_mlp, scale_mlp, gate_mlp = (
        vectors[k] for k in range(6)
    )

    normed_a, inverse_a = layer_norm(tokens_in)
    input_a = (normed_a * (1.0 + scale_attn) + shift_attn).astype(bf16)
    chunks_a = expand(input_a)
    count = len(chunks_a)
    qkv_shift = by_pairs(jnp.stack([qv_offset[0], jnp.zeros_like(qv_offset[0]), qv_offset[1]])[None])
    qkv = joined([(nn(chunk, qkv_matrix) + qkv_shift).astype(bf16) for chunk in chunks_a])
    grad_branch_mlp = (gate_mlp * grad_out).astype(bf16)
    chunks_grad_mlp = expand(grad_branch_mlp)

    attended = attend(qkv)
    branch_attn = (
        owned_sums(lambda chunk: nt(chunk, out_matrix_t), chunked(attended, count)) + vectors[6]
    )
    middle = tokens_in + gate_attn * branch_attn
    normed_m, inverse_m = layer_norm(middle)
    input_m = (normed_m * (1.0 + scale_mlp) + shift_mlp).astype(bf16)
    chunks_m = expand(input_m)
    pre_up = [nn(chunk, up_matrix) + up_offset for chunk in chunks_m]
    hidden = [gelu_tanh(chunk).astype(bf16) for chunk in pre_up]

    grad_pre_up = []
    for grad_chunk, pre_chunk in zip(chunks_grad_mlp, pre_up):
        unused_gelu, gelu_back = jax.vjp(gelu_tanh, pre_chunk)
        grad_pre_up.append(gelu_back(nn(grad_chunk, down_matrix_t))[0].astype(bf16))
    grad_input_m = owned_sums(lambda chunk: nt(chunk, up_matrix), grad_pre_up)
    branch_mlp = owned_sums(lambda chunk: nt(chunk, down_matrix_t), hidden) + vectors[7]
    result_out = middle + gate_mlp * branch_mlp
    grad_gate_mlp = jnp.sum(grad_out * branch_mlp, axis=0)
    grad_pre_full = joined(grad_pre_up)
    up_grad = tn(joined(chunks_m), grad_pre_full).astype(bf16)
    down_grad_t = tn(joined(chunks_grad_mlp), joined(hidden)).astype(bf16)
    up_bias_part = jnp.sum(grad_pre_full, axis=0, dtype=f32)
    mlp_grads = lax.psum_scatter(
        jnp.concatenate([up_grad, down_grad_t], axis=1), "dp", scatter_dimension=0, tiled=True
    ).astype(f32)

    grad_shift_mlp = jnp.sum(grad_input_m, axis=0)
    grad_scale_mlp = jnp.sum(grad_input_m * normed_m, axis=0)
    grad_middle = grad_out + norm_back(grad_input_m * (1.0 + scale_mlp), normed_m, inverse_m)
    grad_gate_attn = jnp.sum(grad_middle * branch_attn, axis=0)
    grad_branch_attn = (gate_attn * grad_middle).astype(bf16)
    chunks_grad_attn = expand(grad_branch_attn)
    grad_attended = joined([nn(chunk, out_matrix_t).astype(bf16) for chunk in chunks_grad_attn])
    grad_qkv = attend_back(qkv, grad_attended)
    out_grad_t = tn(joined(chunks_grad_attn), attended).astype(bf16)
    grad_input_a = owned_sums(lambda chunk: nt(chunk, qkv_matrix), chunked(grad_qkv, count))
    qkv_grad = tn(joined(chunks_a), grad_qkv).astype(bf16)
    attn_grads = lax.psum_scatter(
        jnp.concatenate([qkv_grad, out_grad_t], axis=1), "dp", scatter_dimension=0, tiled=True
    ).astype(f32)
    qkv_bias_part = from_pairs(jnp.sum(grad_qkv, axis=0, dtype=f32)[None])[0]
    grad_shift_attn = jnp.sum(grad_input_a, axis=0)
    grad_scale_attn = jnp.sum(grad_input_a * normed_a, axis=0)
    grad_tokens = grad_middle + norm_back(grad_input_a * (1.0 + scale_attn), normed_a, inverse_a)

    token_sums = jnp.stack(
        [
            grad_shift_attn,
            grad_scale_attn,
            grad_gate_attn,
            grad_shift_mlp,
            grad_scale_mlp,
            grad_gate_mlp,
            jnp.sum(grad_branch_attn, axis=0, dtype=f32),
            jnp.sum(grad_branch_mlp, axis=0, dtype=f32),
        ]
    )
    if mp == 2:
        own = lax.dynamic_slice_in_dim(token_sums, my_mp * width, width, axis=1)
        other = lax.dynamic_slice_in_dim(token_sums, (1 - my_mp) * width, width, axis=1)
        column_sums = own + swap(other)
    else:
        column_sums = lax.psum_scatter(token_sums, "mp", scatter_dimension=1, tiled=True)
    mine = jnp.concatenate(
        [column_sums.reshape(1, -1), qkv_bias_part[0:1], qkv_bias_part[2:3], up_bias_part[None]],
        axis=1,
    )
    everyone = lax.all_gather(mine, "dp", axis=0, tiled=True)
    grad_mod_all = everyone[:, : 6 * width]
    sums = jnp.sum(everyone, axis=0)
    mod_grad = lax.dot_general(
        act_rows.astype(f32), grad_mod_all, (((0,), (0,)), ((), ())), precision=precise
    ).reshape(modulation_weight.shape)
    cond_partial = lax.dot_general(
        grad_mod_all, mod_flat.astype(f32), (((1,), (1,)), ((), ())), precision=precise
    )
    grad_activated = jnp.sum(to_latents(cond_partial), axis=1).reshape(1, model_width)
    unused_silu, silu_back = jax.vjp(jax.nn.silu, cond_float)
    cond_grad = lax.dynamic_slice_in_dim(
        silu_back(grad_activated)[0], my_mp * width, width, axis=1
    )

    share = width // dp
    column_totals = sums[: 10 * width].reshape(10, width)
    column_share = lax.dynamic_slice_in_dim(column_totals, my_dp * share, share, axis=1)
    up_share = lax.dynamic_slice_in_dim(sums[10 * width :], my_dp * (ff // dp), ff // dp)

    qkv_cols = 3 * width
    return (
        result_out.astype(bf16)[None],
        grad_tokens.astype(bf16)[None],
        cond_grad.astype(bf16),
        mod_grad,
        column_share[:6],
        from_pairs(attn_grads[:, :qkv_cols]),
        column_share[8:10],
        attn_grads[:, qkv_cols:].T,
        mlp_grads[:, :ff],
        up_share,
        mlp_grads[:, ff:].T,
        column_share[6:8],
    )


def solution(mesh):
    placed = (
        P("dp", "mp", None),
        P("dp", None),
        P("dp", None, "mp"),
        P(None, ("mp", "dp")),
        P("dp", None, "mp"),
        P(None, ("mp", "dp")),
        P("mp", "dp"),
        P("dp", "mp"),
        P(("mp", "dp")),
        P("mp", "dp"),
        P(None, ("mp", "dp")),
        P("dp", "mp", None),
    )
    return jax.shard_map(
        local,
        mesh=mesh,
        in_specs=placed,
        out_specs=(
            P("dp", "mp", None),
            P("dp", "mp", None),
            P("dp", "mp"),
            P("dp", None, "mp"),
            P(None, ("mp", "dp")),
            P("dp", None, "mp"),
            P(None, ("mp", "dp")),
            P("mp", "dp"),
            P("dp", "mp"),
            P(("mp", "dp")),
            P("mp", "dp"),
            P(None, ("mp", "dp")),
        ),
        check_vma=False,
    )
```

```python
import jax
import jax.numpy as jnp
from jax import lax
from jax.experimental import pallas as pl
from jax.experimental.pallas import tpu as pltpu
from jax.sharding import PartitionSpec as P

HEAD_DIM = 64
PAIR = 2 * HEAD_DIM
TEMPER = HEAD_DIM ** (-0.5)

epsilon = 1e-06
precise = lax.Precision.HIGHEST
f32 = jnp.float32
bf16 = jnp.bfloat16


def layer_norm(values):
    center = values - jnp.mean(values, axis=-1, keepdims=True)
    inverse = lax.rsqrt(jnp.mean(center * center, axis=-1, keepdims=True) + epsilon)
    return (center * inverse, inverse)


def norm_back(grad_normed, normed, inverse):
    first = jnp.mean(grad_normed, axis=-1, keepdims=True)
    second = jnp.mean(grad_normed * normed, axis=-1, keepdims=True)
    return inverse * (grad_normed - first - normed * second)


def gelu_tanh(values):
    return jax.nn.gelu(values, approximate=True)


def dot(a, b, contract):
    return lax.dot_general(a, b, (contract, ((), ())), preferred_element_type=f32)


def nn(a, b):
    return dot(a, b, ((1,), (0,)))


def nt(a, b):
    return dot(a, b, ((1,), (1,)))


def tn(a, b):
    return dot(a, b, ((0,), (0,)))


def head_columns(ref, part, head, rows=slice(None)):
    start = part * PAIR + head * HEAD_DIM
    return ref[rows, start : start + HEAD_DIM]


def softmax_columns(scores):
    exponent = jnp.exp(scores - jnp.max(scores, axis=0, keepdims=True))
    return exponent * (1.0 / jnp.sum(exponent, axis=0, keepdims=True))


def attend_kernel(block, qkv_ref, out_ref):
    keys = [head_columns(qkv_ref, 1, h) for h in range(2)]
    values_t = [head_columns(qkv_ref, 2, h).T for h in range(2)]
    for first in range(0, qkv_ref.shape[0], block):
        rows = slice(first, first + block)
        parts = []
        for h in range(2):
            query = head_columns(qkv_ref, 0, h, rows) * TEMPER
            probs = softmax_columns(nt(keys[h], query)).astype(bf16)
            parts.append(nn(values_t[h], probs))
        out_ref[rows, :] = jnp.concatenate(parts, axis=0).T.astype(bf16)


def attend_back_kernel(block, qkv_ref, grad_ref, out_ref, grad_key, grad_value):
    keys = [head_columns(qkv_ref, 1, h) for h in range(2)]
    values = [head_columns(qkv_ref, 2, h) for h in range(2)]
    keys_t = [keys[h].T for h in range(2)]
    for first in range(0, qkv_ref.shape[0], block):
        rows = slice(first, first + block)
        parts = []
        for h in range(2):
            query = head_columns(qkv_ref, 0, h, rows) * TEMPER
            grad = grad_ref[rows, h * HEAD_DIM : (h + 1) * HEAD_DIM]
            probs = softmax_columns(nt(keys[h], query))
            grad_probs = nt(values[h], grad)
            inner = jnp.sum(probs * grad_probs, axis=0, keepdims=True)
            grad_scores = (probs * (grad_probs - inner)).astype(bf16)
            value_part = nn(probs.astype(bf16), grad)
            key_part = nn(grad_scores, query)
            if first == 0:
                grad_value[h] = value_part
                grad_key[h] = key_part
            else:
                grad_value[h] += value_part
                grad_key[h] += key_part
            parts.append(nn(keys_t[h], grad_scores))
        out_ref[rows, :PAIR] = (jnp.concatenate(parts, axis=0).T * TEMPER).astype(bf16)
    out_ref[:, PAIR : 2 * PAIR] = jnp.concatenate([grad_key[0], grad_key[1]], axis=1).astype(bf16)
    out_ref[:, 2 * PAIR :] = jnp.concatenate([grad_value[0], grad_value[1]], axis=1).astype(bf16)


def attend(qkv):
    tokens, width = qkv.shape
    pairs = width // (3 * PAIR)
    block = min(256, tokens)

    def body(qkv_ref, out_ref):
        attend_kernel(block, qkv_ref, out_ref)

    return pl.pallas_call(
        body,
        grid=(pairs,),
        in_specs=[pl.BlockSpec((tokens, 3 * PAIR), lambda p: (0, p))],
        out_specs=pl.BlockSpec((tokens, PAIR), lambda p: (0, p)),
        out_shape=jax.ShapeDtypeStruct((tokens, pairs * PAIR), bf16),
        compiler_params=pltpu.CompilerParams(vmem_limit_bytes=40 * 2**20),
        cost_estimate=pl.CostEstimate(
            flops=16 * pairs * tokens * tokens * PAIR,
            bytes_accessed=8 * tokens * pairs * PAIR,
            transcendentals=2 * pairs * tokens * tokens,
        ),
        name="attend",
    )(qkv)


def attend_back(qkv, grad):
    tokens, width = qkv.shape
    pairs = width // (3 * PAIR)
    block = min(256, tokens)

    def body(*refs):
        attend_back_kernel(block, *refs)

    return pl.pallas_call(
        body,
        grid=(pairs,),
        in_specs=[
            pl.BlockSpec((tokens, 3 * PAIR), lambda p: (0, p)),
            pl.BlockSpec((tokens, PAIR), lambda p: (0, p)),
        ],
        out_specs=pl.BlockSpec((tokens, 3 * PAIR), lambda p: (0, p)),
        out_shape=jax.ShapeDtypeStruct((tokens, width), bf16),
        scratch_shapes=[
            pltpu.VMEM((2, tokens, HEAD_DIM), f32),
            pltpu.VMEM((2, tokens, HEAD_DIM), f32),
        ],
        compiler_params=pltpu.CompilerParams(vmem_limit_bytes=40 * 2**20),
        cost_estimate=pl.CostEstimate(
            flops=40 * pairs * tokens * tokens * PAIR,
            bytes_accessed=14 * tokens * pairs * PAIR,
            transcendentals=2 * pairs * tokens * tokens,
        ),
        name="attend_back",
    )(qkv, grad)


def by_pairs(matrix):
    rows, parts, width = matrix.shape
    split = matrix.reshape(rows, parts, width // PAIR, PAIR)
    return jnp.swapaxes(split, 1, 2).reshape(rows, parts * width)


def from_pairs(matrix):
    rows, width = matrix.shape
    split = matrix.reshape(rows, width // (3 * PAIR), 3, PAIR)
    return jnp.swapaxes(split, 1, 2).reshape(rows, 3, width // 3)


def swap(values):
    return lax.ppermute(values, "mp", [(0, 1), (1, 0)])


def expand(values):
    if lax.axis_size("mp") == 2:
        return [values, swap(values)]
    return [lax.all_gather(values, "mp", axis=0, tiled=True)]


def owned_sums(function, chunks):
    if lax.axis_size("mp") == 2:
        received = swap(function(chunks[1]).astype(bf16))
        return function(chunks[0]) + received.astype(f32)
    return lax.psum_scatter(
        function(chunks[0]).astype(bf16), "mp", scatter_dimension=0, tiled=True
    ).astype(f32)


def chunked(values, count):
    return jnp.split(values, count, axis=0) if count > 1 else [values]


def joined(chunks):
    return jnp.concatenate(chunks, axis=0) if len(chunks) > 1 else chunks[0]


def to_latents(values):
    dp, mp = lax.axis_size("dp"), lax.axis_size("mp")
    width = values.shape[1]
    repeated = jnp.broadcast_to(values[:, None], (dp, mp, width)).reshape(dp * mp, width)
    received = lax.all_to_all(repeated, ("dp", "mp"), 0, 0, tiled=True)
    return received.reshape(dp, mp, width)


def local(
    latents,
    condition,
    modulation_weight,
    modulation_bias,
    query_key_value_weight,
    query_value_bias,
    attention_output_weight,
    up_projection_weight,
    up_projection_bias,
    down_projection_weight,
    projection_row_bias,
    cotangent,
):
    mp, dp = lax.axis_size("mp"), lax.axis_size("dp")
    my_dp, my_mp = lax.axis_index("dp"), lax.axis_index("mp")
    model_width = latents.shape[2]
    width = model_width // mp
    rows = model_width // dp
    ff = up_projection_weight.shape[1]
    tokens_in = latents[0].astype(f32)
    grad_out = cotangent[0].astype(f32)
    cond_float = condition.astype(f32)
    activated = jax.nn.silu(cond_float).astype(bf16)

    small_parts = [
        activated,
        modulation_bias.reshape(1, -1),
        query_value_bias.reshape(1, -1),
        up_projection_bias.reshape(1, -1),
        projection_row_bias.reshape(1, -1),
    ]
    bounds = []
    for part in small_parts:
        start = bounds[-1][1] if bounds else 0
        bounds.append((start, start + part.shape[1]))
    small = lax.all_gather(jnp.concatenate(small_parts, axis=1), "dp", axis=0, tiled=True)
    small_out = [small[:, a:b] for a, b in bounds]

    def bias_rows(gathered, count):
        split = gathered.reshape(dp, count, -1)
        return jnp.swapaxes(split, 0, 1).reshape(count, -1).astype(f32)

    mod_offset = bias_rows(small_out[1], 6)
    qv_offset = bias_rows(small_out[2], 2)
    up_offset = bias_rows(small_out[3], 1)
    row_offset = bias_rows(small_out[4], 2)
    act_rows = lax.dynamic_slice_in_dim(small_out[0], my_dp * rows, rows, axis=1)

    packed = jnp.concatenate([by_pairs(query_key_value_weight), attention_output_weight.T], axis=1)
    attn_full = lax.all_gather(packed, "dp", axis=0, tiled=True)
    qkv_matrix = attn_full[:, : 3 * width]
    out_matrix_t = attn_full[:, 3 * width :]
    packed = jnp.concatenate([up_projection_weight, down_projection_weight.T], axis=1)
    packed, attn_full = lax.optimization_barrier((packed, attn_full))
    mlp_full = lax.all_gather(packed, "dp", axis=0, tiled=True)
    up_matrix = mlp_full[:, :ff]
    down_matrix_t = mlp_full[:, ff:]

    mod_flat = modulation_weight.reshape(rows, -1)
    mod_partial = nn(act_rows, mod_flat)
    extra = jnp.concatenate([mod_offset.reshape(1, -1), row_offset.reshape(1, -1)], axis=1)
    payload = jnp.pad(mod_partial, ((0, 0), (0, 2 * width))) + jnp.where(my_dp == 0, extra, 0.0)
    arrived = jnp.sum(to_latents(payload), axis=0).reshape(mp, 8, width)
    vectors = jnp.swapaxes(arrived, 0, 1).reshape(8, 1, model_width)
    shift_attn, scale_attn, gate_attn, shift_mlp, scale_mlp, gate_mlp = (
        vectors[k] for k in range(6)
    )

    normed_a, inverse_a = layer_norm(tokens_in)
    input_a = (normed_a * (1.0 + scale_attn) + shift_attn).astype(bf16)
    chunks_a = expand(input_a)
    count = len(chunks_a)
    qkv_shift = by_pairs(jnp.stack([qv_offset[0], jnp.zeros_like(qv_offset[0]), qv_offset[1]])[None])
    qkv = joined([(nn(chunk, qkv_matrix) + qkv_shift).astype(bf16) for chunk in chunks_a])
    grad_branch_mlp = (gate_mlp * grad_out).astype(bf16)
    grad_branch_mlp, qkv = lax.optimization_barrier((grad_branch_mlp, qkv))
    chunks_grad_mlp = expand(grad_branch_mlp)

    attended = attend(qkv)
    attended, chunks_grad_mlp = lax.optimization_barrier((attended, chunks_grad_mlp))
    branch_attn = (
        owned_sums(lambda chunk: nt(chunk, out_matrix_t), chunked(attended, count)) + vectors[6]
    )
    middle = tokens_in + gate_attn * branch_attn
    normed_m, inverse_m = layer_norm(middle)
    input_m = (normed_m * (1.0 + scale_mlp) + shift_mlp).astype(bf16)
    chunks_m = expand(input_m)
    pre_up = [nn(chunk, up_matrix) + up_offset for chunk in chunks_m]
    hidden = [gelu_tanh(chunk).astype(bf16) for chunk in pre_up]

    grad_pre_up = []
    for grad_chunk, pre_chunk in zip(chunks_grad_mlp, pre_up):
        unused_gelu, gelu_back = jax.vjp(gelu_tanh, pre_chunk)
        grad_pre_up.append(gelu_back(nn(grad_chunk, down_matrix_t))[0].astype(bf16))
    grad_input_m = owned_sums(lambda chunk: nt(chunk, up_matrix), grad_pre_up)
    grad_pre_full = joined(grad_pre_up)
    up_grad = tn(joined(chunks_m), grad_pre_full).astype(bf16)
    down_grad_t = tn(joined(chunks_grad_mlp), joined(hidden)).astype(bf16)
    up_bias_part = jnp.sum(grad_pre_full, axis=0, dtype=f32)
    mlp_packed = jnp.concatenate([up_grad, down_grad_t], axis=1)

    grad_shift_mlp = jnp.sum(grad_input_m, axis=0)
    grad_scale_mlp = jnp.sum(grad_input_m * normed_m, axis=0)
    grad_middle = grad_out + norm_back(grad_input_m * (1.0 + scale_mlp), normed_m, inverse_m)
    grad_gate_attn = jnp.sum(grad_middle * branch_attn, axis=0)
    grad_branch_attn = (gate_attn * grad_middle).astype(bf16)
    chunks_grad_attn = expand(grad_branch_attn)
    grad_attended = joined([nn(chunk, out_matrix_t).astype(bf16) for chunk in chunks_grad_attn])
    grad_attended, mlp_packed, hidden = lax.optimization_barrier(
        (grad_attended, mlp_packed, hidden)
    )
    mlp_grads = lax.psum_scatter(mlp_packed, "dp", scatter_dimension=0, tiled=True)
    branch_mlp = owned_sums(lambda chunk: nt(chunk, down_matrix_t), hidden) + vectors[7]
    result_out = middle + gate_mlp * branch_mlp
    grad_gate_mlp = jnp.sum(grad_out * branch_mlp, axis=0)
    grad_qkv = attend_back(qkv, grad_attended)
    grad_qkv, mlp_grads = lax.optimization_barrier((grad_qkv, mlp_grads))
    out_grad_t = tn(joined(chunks_grad_attn), attended).astype(bf16)
    grad_input_a = owned_sums(lambda chunk: nt(chunk, qkv_matrix), chunked(grad_qkv, count))
    qkv_grad = tn(joined(chunks_a), grad_qkv).astype(bf16)
    attn_packed = jnp.concatenate([qkv_grad, out_grad_t], axis=1)
    attn_grads = lax.psum_scatter(attn_packed, "dp", scatter_dimension=0, tiled=True).astype(f32)
    mlp_grads = mlp_grads.astype(f32)
    qkv_bias_part = from_pairs(jnp.sum(grad_qkv, axis=0, dtype=f32)[None])[0]
    grad_shift_attn = jnp.sum(grad_input_a, axis=0)
    grad_scale_attn = jnp.sum(grad_input_a * normed_a, axis=0)
    grad_tokens = grad_middle + norm_back(grad_input_a * (1.0 + scale_attn), normed_a, inverse_a)

    token_sums = jnp.stack(
        [
            grad_shift_attn,
            grad_scale_attn,
            grad_gate_attn,
            grad_shift_mlp,
            grad_scale_mlp,
            grad_gate_mlp,
            jnp.sum(grad_branch_attn, axis=0, dtype=f32),
            jnp.sum(grad_branch_mlp, axis=0, dtype=f32),
        ]
    )
    if mp == 2:
        own = lax.dynamic_slice_in_dim(token_sums, my_mp * width, width, axis=1)
        other = lax.dynamic_slice_in_dim(token_sums, (1 - my_mp) * width, width, axis=1)
        column_sums = own + swap(other)
    else:
        column_sums = lax.psum_scatter(token_sums, "mp", scatter_dimension=1, tiled=True)
    mine = jnp.concatenate(
        [column_sums.reshape(1, -1), qkv_bias_part[0:1], qkv_bias_part[2:3], up_bias_part[None]],
        axis=1,
    )
    everyone = lax.all_gather(mine, "dp", axis=0, tiled=True)
    grad_mod_all = everyone[:, : 6 * width]
    sums = jnp.sum(everyone, axis=0)
    mod_grad = lax.dot_general(
        act_rows.astype(f32), grad_mod_all, (((0,), (0,)), ((), ())), precision=precise
    ).reshape(modulation_weight.shape)
    cond_partial = lax.dot_general(
        grad_mod_all, mod_flat.astype(f32), (((1,), (1,)), ((), ())), precision=precise
    )
    grad_activated = jnp.sum(to_latents(cond_partial), axis=1).reshape(1, model_width)
    unused_silu, silu_back = jax.vjp(jax.nn.silu, cond_float)
    cond_grad = lax.dynamic_slice_in_dim(
        silu_back(grad_activated)[0], my_mp * width, width, axis=1
    )

    share = width // dp
    column_totals = sums[: 10 * width].reshape(10, width)
    column_share = lax.dynamic_slice_in_dim(column_totals, my_dp * share, share, axis=1)
    up_share = lax.dynamic_slice_in_dim(sums[10 * width :], my_dp * (ff // dp), ff // dp)

    qkv_cols = 3 * width
    return (
        result_out.astype(bf16)[None],
        grad_tokens.astype(bf16)[None],
        cond_grad.astype(bf16),
        mod_grad,
        column_share[:6],
        from_pairs(attn_grads[:, :qkv_cols]),
        column_share[8:10],
        attn_grads[:, qkv_cols:].T,
        mlp_grads[:, :ff],
        up_share,
        mlp_grads[:, ff:].T,
        column_share[6:8],
    )


def solution(mesh):
    placed = (
        P("dp", "mp", None),
        P("dp", None),
        P("dp", None, "mp"),
        P(None, ("mp", "dp")),
        P("dp", None, "mp"),
        P(None, ("mp", "dp")),
        P("mp", "dp"),
        P("dp", "mp"),
        P(("mp", "dp")),
        P("mp", "dp"),
        P(None, ("mp", "dp")),
        P("dp", "mp", None),
    )
    return jax.shard_map(
        local,
        mesh=mesh,
        in_specs=placed,
        out_specs=(
            P("dp", "mp", None),
            P("dp", "mp", None),
            P("dp", "mp"),
            P("dp", None, "mp"),
            P(None, ("mp", "dp")),
            P("dp", None, "mp"),
            P(None, ("mp", "dp")),
            P("mp", "dp"),
            P("dp", "mp"),
            P(("mp", "dp")),
            P("mp", "dp"),
            P(None, ("mp", "dp")),
        ),
        check_vma=False,
    )
```
